32 devices in a mesh: segment: 2 (over x), tm: 4 (over z), space: 4 (over y, core).
Axes of the slice: x: 2, y: 2, z: 4, core: 2. Of those that a mesh axis runs over, the one named last changes fastest.
Arguments:
- video_clips: float32 [2, 8, 16, 32, 128], P(None, 'tm', 'space'), may hold values from -6 to 6
- conv_weights: float32 [2, 3456, 128], P('segment'), may hold values from -0.109375 to 0.109375
Outputs:
- weight_grads: float32 [2, 3456, 128], P('segment')
The draws below stay inside these ranges and needn't reach their ends.
All inputs are finite; a program needn't handle non-finite values.
Results may differ from the reference program's by a relative error of at most 0.000091.
Values sent between devices are 32-bit elements; how exact they have to be, the bound alone decides.
No kernel may reach another device: no remote copies, remote signals or barrier semaphores. Data moves between devices by JAX's collectives and lax.ppermute only.
A program may use at most 64 MiB of HBM per device.

```python
import jax
import jax.numpy as jnp
from jax import lax

C = 128
CLIPS = 2
COLS = 32
FRAMES = 8
ROWS = 16


def levels(stream_key, dims, shards, least, largest):
    loudness = 1.0
    for dim, shards_of in shards:
        steps = jax.random.uniform(jax.random.fold_in(jax.random.fold_in(stream_key, 6), dim), (shards_of,), jnp.float32, least / len(shards), largest / len(shards))
        loudness = loudness * jnp.repeat(jnp.exp(steps), dims[dim] // shards_of).reshape((-1,) + (1,) * (len(dims) - 1 - dim))
    return loudness


def normal_values(rng, dims, width, bound, split=(), kind=jnp.bfloat16):
    array = jax.random.normal(rng, dims, jnp.float32) * width
    if len(split) > 0:
        array = levels(rng, dims, split, -0.22, 0.18) * array
    return jnp.clip(array, min=-bound, max=bound).astype(kind)


def setup_inputs(seed: int = 0) -> dict:
    streams_of = jax.random.split(jax.random.key(seed), 3)
    return {
        "video_clips": normal_values(streams_of[0], (CLIPS, FRAMES, ROWS, COLS, C), 1.0, 6.0, ((1, 4), (2, 4)), jnp.float32),
        "conv_weights": normal_values(streams_of[1], (2, 27 * C, C), (27 * C) ** -0.5, 0.109375, ((0, 2),), jnp.float32),
    }


def convolve(field_in, weight):
    kernel = weight.reshape(3, 3, 3, C, C)
    return lax.conv_general_dilated(field_in, kernel, (1, 1, 1), ((2, 0), (1, 1), (1, 1)), dimension_numbers=('NDHWC', 'DHWIO', 'NDHWC'), precision=lax.Precision.HIGHEST)

def reference(video_clips, conv_weights):
    factor = float(CLIPS * FRAMES * ROWS * COLS) ** (-0.5)

    def forward(encoder, decoder):
        return convolve(jax.nn.silu(convolve(video_clips, encoder)), decoder)
    decoded, pullback = jax.vjp(forward, conv_weights[0], conv_weights[1])
    cotangent = (decoded - video_clips) * factor
    grad_encoder, grad_decoder = pullback(cotangent)
    return jnp.stack([grad_encoder, grad_decoder])
```

```python
import functools

import jax
import jax.numpy as jnp
from jax import lax
from jax.experimental import pallas as pl
from jax.experimental.pallas import tpu as pltpu
from jax.sharding import PartitionSpec as P

f32 = jnp.float32
bf16 = jnp.bfloat16
AXES = ("segment", "tm", "space")
VMEM_LIMIT = 56 * 1024 * 1024


def split(x):
    high = x.astype(bf16)
    low = (x - high.astype(f32)).astype(bf16)
    return high, low


def dot(a, b):
    return jnp.dot(a, b, preferred_element_type=f32)


def rotate(x, amount, axis):
    size = x.shape[axis]
    amount = amount % size
    if amount == 0:
        return x
    return jnp.concatenate(
        [lax.slice_in_dim(x, size - amount, size, axis=axis), lax.slice_in_dim(x, 0, size - amount, axis=axis)],
        axis=axis,
    )


def column_triple(x):
    column = lax.broadcasted_iota(jnp.int32, x.shape, x.ndim - 2)
    before = jnp.where(column == 0, 0.0, rotate(x, 1, x.ndim - 2))
    after = jnp.where(column == x.shape[-2] - 1, 0.0, rotate(x, -1, x.ndim - 2))
    return [before, x, after]


def store_triple(high_ref, low_ref, index, x):
    channels = x.shape[-1]
    for i, part in enumerate(column_triple(x)):
        high, low = split(part)
        lanes = pl.ds(i * channels, channels)
        high_ref[index + (slice(None), lanes)] = high
        low_ref[index + (slice(None), lanes)] = low


def activations_kernel(
    dims, at_ref, block_ref, up_ref, down_ref, own_ref, mine_ref, other_ref,
    sent_ref, values_ref,
    xh, xl, lh, ll, ch, cl, weight, weight_t, video, hidden, grads,
):
    tm, own_frames, height, rows_all, columns, channels, factor = dims
    frames = tm * own_frames
    per = height // tm
    cells = frames * columns
    segment, z, p = at_ref[0], at_ref[1], at_ref[2]
    core = lax.rem(p, 2)
    half = own_ref.shape[0] // 2

    def put_weight(which, start, ref, rows, offset):
        step = 128
        for r in range(0, rows, step):
            n = min(step, rows - r)
            high, low = split(ref[pl.ds(offset + r, n), :])
            at = pl.ds(pl.multiple_of(start + r, 16), n)
            weight[which, at, pl.ds(0, channels)] = high
            weight[which, at, pl.ds(channels, channels)] = low

    put_weight(segment, 0, own_ref, own_ref.shape[0], 0)
    put_weight(1 - segment, core * half, mine_ref, half, 0)
    put_weight(1 - segment, (1 - core) * half, other_ref, half, 0)

    for ref in (xh, xl, lh, ll):
        ref[:, 0:2] = jnp.zeros((ref.shape[0], 2) + ref.shape[2:], bf16)
    for ref in (ch, cl):
        ref[:, frames:] = jnp.zeros((ref.shape[0], 2) + ref.shape[2:], bf16)
    values_ref[:, :, 0:2] = jnp.zeros((2, height + 2, 2, columns, 2 * channels), bf16)
    for k in range(tm):
        first = lax.rem(z - k + tm, tm) * own_frames
        for row in range(-3, height + 3):
            if row < 0:
                x = up_ref[k, :, 3 + row]
            elif row < height:
                x = block_ref[k, :, row]
            else:
                x = down_ref[k, :, row - height]
            store_triple(xh, xl, (row + 3, pl.ds(first + 2, own_frames)), x)
            if -1 <= row <= height:
                video[row + 1, pl.ds(first, own_frames)] = x
                high, low = split(x)
                at = pl.ds(first + 2, own_frames)
                values_ref[0, row + 1, at, :, pl.ds(0, channels)] = high
                values_ref[0, row + 1, at, :, pl.ds(channels, channels)] = low

    def convolved(high_ref, low_ref, row, count, which):
        high, low = [], []
        for a in range(3):
            for b in range(3):
                at = (pl.ds(row + b, count), pl.ds(a, frames))
                high.append(high_ref[at].reshape(count * cells, 3 * channels))
                low.append(low_ref[at].reshape(count * cells, 3 * channels))
        both = dot(jnp.concatenate(high, axis=1), weight[which])
        rest = dot(jnp.concatenate(low, axis=1), weight[which, :, pl.ds(0, channels)])
        return both[:, :channels] + both[:, channels:] + rest

    group = 2

    @pl.loop(0, (height + 4) // group)
    def _(i):
        row = i * group
        value = convolved(xh, xl, row, group, 0).reshape(group, frames, columns, channels)
        for j in range(group):
            place = p * height - 2 + row + j
            inside = jnp.logical_and(place >= 0, place < rows_all)
            one = value[j]
            hidden[row + j] = one
            latent = jnp.where(inside, one / (1.0 + jnp.exp(-one)), 0.0)
            store_triple(lh, ll, (row + j, pl.ds(2, frames)), latent)

    for row in range(height + 2):
        values_ref[1, row, pl.ds(2, frames), :, pl.ds(0, channels)] = lh[
            row + 1, pl.ds(2, frames), :, pl.ds(channels, channels)
        ]
        values_ref[1, row, pl.ds(2, frames), :, pl.ds(channels, channels)] = ll[
            row + 1, pl.ds(2, frames), :, pl.ds(channels, channels)
        ]

    for j in range(per + 2):
        row = z * per - 1 + j
        decoded = convolved(lh, ll, row + 1, 1, 1).reshape(frames, columns, channels)
        place = p * height + row
        inside = jnp.logical_and(place >= 0, place < rows_all)
        cotangent = jnp.where(inside, (decoded - video[row + 1]) * factor, 0.0)
        store_triple(ch, cl, (j, pl.ds(0, frames)), cotangent)
        if 1 <= j <= per:
            grads[1, :, pl.ds((j - 1) * cells, cells)] = cotangent.reshape(cells, channels).T

    for tap in range(9):
        for e in range(3):
            at = pl.ds((tap * 3 + 2 - e) * channels, channels)
            to = pl.ds((tap * 3 + e) * channels, channels)
            for part in range(2):
                lanes = pl.ds(part * channels, channels)
                weight_t[to, lanes] = weight[1, at, lanes].astype(f32).T.astype(bf16)

    for j in range(per):
        high, low = [], []
        for a in range(3):
            for b in range(3):
                at = (j + 2 - b, pl.ds(2 - a, frames))
                high.append(ch[at].reshape(cells, 3 * channels))
                low.append(cl[at].reshape(cells, 3 * channels))
        both = dot(jnp.concatenate(high, axis=1), weight_t[...])
        rest = dot(jnp.concatenate(low, axis=1), weight_t[:, pl.ds(0, channels)])
        grad_latent = both[:, :channels] + both[:, channels:] + rest
        value = hidden[z * per + j + 2].reshape(cells, channels)
        sigmoid = 1.0 / (1.0 + jnp.exp(-value))
        grad = grad_latent * (sigmoid * (1.0 + value * (1.0 - sigmoid)))
        grads[0, :, pl.ds(j * cells, cells)] = grad.T

    part = channels // tm
    for k in range(tm):
        target = lax.rem(z + k, tm)
        at = pl.ds(pl.multiple_of(target * part, part), part)
        for which in range(2):
            sent_ref[k, which] = grads[which, at, :]


def weights_kernel(dims, at_ref, *refs):
    tm, own_frames, height, rows_all, columns, channels, pairs = dims
    pieces, (values_ref, keep_ref, send_ref, field) = refs[:tm], refs[tm:]
    frames = tm * own_frames
    per = height // tm
    cells = frames * columns
    part = channels // tm
    share = part // 2
    width = share // pairs
    segment, z, p = at_ref[0], at_ref[1], at_ref[2]
    core = lax.rem(p, 2)
    y = lax.div(p, 2)

    for relative in range(2):
        which = segment if relative == 0 else 1 - segment
        for k in range(tm):
            first = lax.rem(z - k + tm, tm) * per
            ordered = []
            for side in range(2):
                its = core if side == 0 else 1 - core
                for step in range(pairs):
                    its_y = lax.rem(y + step, pairs)
                    start = its * share + its_y * width
                    ordered.append(pieces[k][which, pl.ds(start, width), :])
            x = jnp.concatenate(ordered, axis=0)
            for j in range(per):
                row = x[:, j * cells : (j + 1) * cells]
                column = lax.rem(lax.broadcasted_iota(jnp.int32, row.shape, 1), columns)
                after = jnp.where(column == columns - 1, 0.0, rotate(row, -1, 1))
                before = jnp.where(column == 0, 0.0, rotate(row, 1, 1))
                high, low = split(jnp.concatenate([after, row, before], axis=0))
                field[relative, first + j, pl.ds(0, 3 * part), :] = high
                field[relative, first + j, pl.ds(3 * part, 3 * part), :] = low

    for relative in range(2):
        which = segment if relative == 0 else 1 - segment
        left = jnp.concatenate([field[relative, row] for row in range(height)], axis=1)
        for a in range(3):
            for b in range(3):
                right = values_ref[which, pl.ds(b, height), pl.ds(a, frames)]
                product = dot(left, right.reshape(height * cells, 2 * channels))
                full = 3 * part
                total = product[:full, :channels] + product[:full, channels:] + product[full:, :channels]
                for e in range(3):
                    tap = (a * 3 + b) * 3 + e
                    for side, ref in enumerate((keep_ref, send_ref)):
                        for step in range(pairs):
                            start = e * part + side * share + step * width
                            ref[relative, step, tap] = total[start : start + width]


def assembled_kernel(dims, at_ref, kept_ref, came_ref, out_ref):
    tm, pairs, channels = dims
    segment, z, p = at_ref[0], at_ref[1], at_ref[2]
    core = lax.rem(p, 2)
    y = lax.div(p, 2)
    taps = kept_ref.shape[2]
    for tap in range(taps):
        parts = []
        for target in range(tm):
            k = lax.rem(z - target + tm, tm)
            for side in range(2):
                for its_y in range(pairs):
                    step = lax.rem(y - its_y + pairs, pairs)
                    kept = kept_ref[step, k, tap]
                    came = came_ref[step, k, tap]
                    parts.append(jnp.where(core == side, kept, came))
        out_ref[pl.ds(tap * channels, channels), :] = jnp.concatenate(parts, axis=0).T


def vmem(shape, dtype):
    return pltpu.VMEM(shape, dtype)


def call(kernel, shapes, scratch, count, flops):
    single = not isinstance(shapes, list)
    space = pl.BlockSpec(memory_space=pltpu.VMEM)
    return pl.pallas_call(
        kernel,
        out_shape=shapes,
        in_specs=[pl.BlockSpec(memory_space=pltpu.SMEM)] + [space] * count,
        out_specs=space if single else [space] * len(shapes),
        scratch_shapes=scratch,
        compiler_params=pltpu.CompilerParams(vmem_limit_bytes=VMEM_LIMIT),
        cost_estimate=pl.CostEstimate(flops=flops, bytes_accessed=8_000_000, transcendentals=0),
    )


def make_local(sizes):
    segments, tm, space = sizes["segment"], sizes["tm"], sizes["space"]
    pairs = space // 2

    def send(x, move):
        route = []
        for s in range(segments):
            for t in range(tm):
                for p in range(space):
                    target = move(s, t, p)
                    if target is not None:
                        s2, t2, p2 = target
                        route.append(((s * tm + t) * space + p, (s2 * tm + t2) * space + p2))
        return lax.ppermute(x, AXES, route)

    def later(k):
        return lambda s, t, p: (s, (t + k) % tm, p)

    def across(flip, step):
        return lambda s, t, p: (s ^ flip, t, ((p // 2 + step) % pairs) * 2 + p % 2)

    def swap_section(s, t, p):
        return (1 - s, t, p)

    def swap_core(s, t, p):
        return (s, t, p ^ 1)

    def row_down(s, t, p):
        return (s, t, p + 1) if p + 1 < space else None

    def row_up(s, t, p):
        return (s, t, p - 1) if p > 0 else None

    def local(video_clips, conv_weights):
        clips, own_frames, height, columns, channels = video_clips.shape
        frames = tm * own_frames
        rows_all = height * space
        per = height // tm
        cells = frames * columns
        factor = float(clips * frames * rows_all * columns) ** (-0.5)
        segment = lax.axis_index("segment")
        z = lax.axis_index("tm")
        p = lax.axis_index("space")
        at = jnp.stack([segment, z, p]).astype(jnp.int32)
        own = conv_weights[0]
        taps = own.shape[0] // channels
        half = own.shape[0] // 2

        mine = send(lax.dynamic_slice_in_dim(own, (p % 2) * half, half, 0), swap_section)
        clip = lax.dynamic_index_in_dim(video_clips, segment, 0, keepdims=False)
        block = jnp.stack([clip] + [send(clip, later(k)) for k in range(1, tm)])
        up = send(block[:, :, height - 3 :], row_down)
        down = send(block[:, :, :3], row_up)
        other = send(mine, swap_core)

        part = channels // tm
        full = 3 * channels
        sent, values = call(
            functools.partial(
                activations_kernel, (tm, own_frames, height, rows_all, columns, channels, factor)
            ),
            [
                jax.ShapeDtypeStruct((tm, 2, part, per * cells), f32),
                jax.ShapeDtypeStruct((2, height + 2, frames + 2, columns, 2 * channels), bf16),
            ],
            [vmem((height + 6, frames + 2, columns, full), bf16)] * 2
            + [vmem((height + 4, frames + 2, columns, full), bf16)] * 2
            + [vmem((per + 2, frames + 2, columns, full), bf16)] * 2
            + [
                vmem((2, own.shape[0], 2 * channels), bf16),
                vmem((own.shape[0], 2 * channels), bf16),
                vmem((height + 2, frames, columns, channels), f32),
                vmem((height + 4, frames, columns, channels), f32),
                vmem((2, channels, per * cells), f32),
            ],
            6,
            6 * own.shape[0] * channels * cells * (height + 4 + 2 * per + 2),
        )(at, block, up, down, own, mine, other)

        pieces = [sent[0]] + [send(sent[k], later(k)) for k in range(1, tm)]
        width = part // (2 * pairs)
        shape = jax.ShapeDtypeStruct((2, pairs, taps, width, channels), f32)
        keep, give = call(
            functools.partial(
                weights_kernel, (tm, own_frames, height, rows_all, columns, channels, pairs)
            ),
            [shape, shape],
            [vmem((2, height, 6 * part, cells), bf16)],
            tm + 1,
            16 * taps * part * height * cells * channels,
        )(at, *pieces, values)

        both = keep + send(give, swap_core)
        total = both[0, 0]
        for flip in range(2):
            for step in range(pairs):
                if flip or step:
                    total = total + send(both[flip, step], across(flip, step))

        gathered = jnp.stack([total] + [send(total, later(k)) for k in range(1, tm)])
        gathered = jnp.stack([gathered] + [send(gathered, across(0, k)) for k in range(1, pairs)])
        came = send(gathered, swap_core)
        out = call(
            functools.partial(assembled_kernel, (tm, pairs, channels)),
            jax.ShapeDtypeStruct(own.shape, f32),
            [],
            2,
            0,
        )(at, gathered, came)
        return out[None]

    return local


def solution(mesh):
    return jax.shard_map(
        make_local(dict(mesh.shape)),
        mesh=mesh,
        in_specs=(P(None, "tm", "space", None, None), P("segment", None, None)),
        out_specs=P("segment", None, None),
        check_vma=False,
    )
```

```python
import functools

import jax
import jax.numpy as jnp
from jax import lax
from jax.experimental import pallas as pl
from jax.experimental.pallas import tpu as pltpu
from jax.sharding import PartitionSpec as P

f32 = jnp.float32
bf16 = jnp.bfloat16
AXES = ("segment", "tm", "space")
MIB = 1024 * 1024


def split(x):
    high = x.astype(bf16)
    low = (x - high.astype(f32)).astype(bf16)
    return high, low


def dot(a, b):
    return jnp.dot(a, b, preferred_element_type=f32)


def rotate(x, amount, axis):
    size = x.shape[axis]
    amount = amount % size
    if amount == 0:
        return x
    return jnp.concatenate(
        [lax.slice_in_dim(x, size - amount, size, axis=axis), lax.slice_in_dim(x, 0, size - amount, axis=axis)],
        axis=axis,
    )


def store_split(high_ref, low_ref, index, x):
    high, low = split(x)
    high_ref[index] = high
    low_ref[index] = low


def put_taps(to_ref, tap, x):
    channels = x.shape[-1]
    rows = pl.ds((tap // 3) * channels, channels)
    high, low = split(x)
    to_ref[rows, pl.ds((tap % 3) * channels, channels)] = high
    to_ref[rows, pl.ds((tap % 3 + 3) * channels, channels)] = low


def shifted_sum(y, columns, channels, flip):
    parts = [y[:, i * channels : (i + 1) * channels].reshape(-1, columns, channels) for i in range(3)]
    if flip:
        parts = parts[::-1]
    column = lax.broadcasted_iota(jnp.int32, parts[0].shape, 1)
    first = jnp.where(column == 0, 0.0, rotate(parts[0], 1, 1))
    last = jnp.where(column == columns - 1, 0.0, rotate(parts[2], -1, 1))
    return parts[1] + first + last


def convolved(high_ref, low_ref, places, count, dims, weight_ref, flip=False):
    frames, columns, channels = dims
    high, low = [], []
    for row, a in places:
        at = (pl.ds(row, count), pl.ds(a, frames))
        high.append(high_ref[at].reshape(count * frames * columns, channels))
        low.append(low_ref[at].reshape(count * frames * columns, channels))
    full = 3 * channels
    both = dot(jnp.concatenate(high, axis=1), weight_ref[...])
    rest = dot(jnp.concatenate(low, axis=1), weight_ref[:, pl.ds(0, full)])
    y = both[:, :full] + both[:, full:] + rest
    return shifted_sum(y, columns, channels, flip).reshape(count, frames, columns, channels)


def received_taps(core, refs, tap, channels):
    mine_ref, other_ref, mine_late_ref, other_late_ref = refs
    if tap < 18:
        at = pl.ds((tap % 9) * channels, channels)
        return jnp.where(core == tap // 9, mine_ref[at, :], other_ref[at, :])
    half = mine_late_ref.shape[0]
    start, parts = (tap - 18) * channels, []
    while start < (tap - 17) * channels:
        side = start // half
        stop = min((side + 1) * half, (tap - 17) * channels)
        at = pl.ds(start - side * half, stop - start)
        parts.append(jnp.where(core == side, mine_late_ref[at, :], other_late_ref[at, :]))
        start = stop
    return parts[0] if len(parts) == 1 else jnp.concatenate(parts, axis=0)


def field_rows(high_ref, low_ref, row, shape, weight_ref):
    places = [(row + b, a) for a in range(3) for b in range(3)]
    return convolved(high_ref, low_ref, places, 1, shape, weight_ref)[0]


def store_latent(high_ref, low_ref, row, place, rows_all, value):
    latent = value / (1.0 + jnp.exp(-value))
    inside = jnp.logical_and(place >= 0, place < rows_all)
    frames = value.shape[0]
    store_split(high_ref, low_ref, (row, pl.ds(2, frames)), jnp.where(inside, latent, 0.0))


def missing_row(z, i, height, per):
    below = jnp.maximum(z * per - 1, 0)
    row = jnp.where(i < below, 1 + i, z * per + per + 4 + i - below)
    return jnp.minimum(row, height + 3)


def latents_kernel(dims, xh, xl, encoder, lh, ll):
    tm, own_frames, height, rows_all, columns, channels, factor = dims
    frames = tm * own_frames
    per = height // tm
    z, p = lax.axis_index("tm"), lax.axis_index("space")
    for ref in (lh, ll):
        ref[:, 0:2] = jnp.zeros((ref.shape[0], 2) + ref.shape[2:], bf16)
    for i in range(lh.shape[0]):
        row = missing_row(z, i, height, per)
        value = field_rows(xh, xl, row, (frames, columns, channels), encoder)
        store_latent(lh, ll, i, p * height + row - 2, rows_all, value)


def pick_kernel(video_ref, weights_ref, early_ref, late_ref, clip_ref, sems):
    early, late = early_ref.shape[0], late_ref.shape[0]
    segment, core = lax.axis_index("segment"), lax.rem(lax.axis_index("space"), 2)
    copies = [
        pltpu.make_async_copy(weights_ref.at[0, pl.ds(core * early, early)], early_ref, sems.at[0]),
        pltpu.make_async_copy(weights_ref.at[0, pl.ds(2 * early + core * late, late)], late_ref, sems.at[1]),
        pltpu.make_async_copy(video_ref.at[segment], clip_ref, sems.at[2]),
    ]
    for copy in copies:
        copy.start()
    for copy in copies:
        copy.wait()


def activations_kernel(
    dims, block_ref, inner_ref, outer_ref, own_ref, *refs
):
    tm, own_frames, height, rows_all, columns, channels, factor = dims
    came_refs, sent_refs = refs[:4], refs[4 : 4 + tm]
    xh, xl, lh, ll, encoder, video, decoder, turned, ch, cl, hidden, grads = refs[4 + tm :]
    frames = tm * own_frames
    per = height // tm
    cells = frames * columns
    shape = (frames, columns, channels)
    segment, z, p = (lax.axis_index(name) for name in AXES)
    core = lax.rem(p, 2)

    for tap in range(27):
        own = own_ref[pl.ds(tap * channels, channels), :]
        came = received_taps(core, came_refs, tap, channels)
        put_taps(encoder, tap, jnp.where(segment == 0, own, came))
        block = jnp.where(segment == 0, came, own)
        put_taps(decoder, tap, block)
        put_taps(turned, tap, block.T)
    for ref in (xh, xl, lh, ll):
        ref[:, 0:2] = jnp.zeros((ref.shape[0], 2) + ref.shape[2:], bf16)
    for ref in (ch, cl):
        ref[:, frames:] = jnp.zeros((ref.shape[0], 2) + ref.shape[2:], bf16)

    for k in range(tm):
        first = k * own_frames
        for row in range(-3, height + 3):
            if row < 0:
                x = jnp.where(core == 0, outer_ref[k, :, 3 + row], inner_ref[k, :, 3 + row])
            elif row < height:
                x = block_ref[k, :, row]
            else:
                x = jnp.where(core == 0, inner_ref[k, :, row - height], outer_ref[k, :, row - height])
            store_split(xh, xl, (row + 3, pl.ds(first + 2, own_frames)), x)
            if -1 <= row <= height:
                video[row + 1, pl.ds(first, own_frames)] = x

    start = z * per
    for row in range(per + 4):
        value = field_rows(xh, xl, start + row, shape, encoder)
        if 2 <= row < per + 2:
            hidden[row - 2] = value
        store_latent(lh, ll, start + row, p * height + start + row - 2, rows_all, value)

    for j in range(per + 2):
        row = z * per - 1 + j
        decoded = field_rows(lh, ll, row + 1, shape, decoder)
        place = p * height + row
        inside = jnp.logical_and(place >= 0, place < rows_all)
        cotangent = jnp.where(inside, (decoded - video[row + 1]) * factor, 0.0)
        store_split(ch, cl, (j, pl.ds(0, frames)), cotangent)
        if 1 <= j <= per:
            grads[1, :, pl.ds((j - 1) * cells, cells)] = cotangent.reshape(cells, channels).T

    for j in range(per):
        places = [(j + 2 - b, 2 - a) for a in range(3) for b in range(3)]
        grad_latent = convolved(ch, cl, places, 1, shape, turned, flip=True)[0]
        value = hidden[j]
        sigmoid = 1.0 / (1.0 + jnp.exp(-value))
        grad = grad_latent * (sigmoid * (1.0 + value * (1.0 - sigmoid)))
        grads[0, :, pl.ds(j * cells, cells)] = grad.reshape(cells, channels).T

    part = channels // tm
    for k, ref in enumerate(sent_refs):
        target = lax.rem(z + k, tm)
        at = pl.ds(pl.multiple_of(target * part, part), part)
        for which in range(2):
            ref[which] = grads[which, at, :]


def weights_kernel(dims, *refs):
    tm, own_frames, height, rows_all, columns, channels, pairs = dims
    pieces = refs[:tm]
    xh, xl, own_high, own_low, more_high, more_low, keep_ref, send_ref, field, lh, ll = refs[tm:]
    frames = tm * own_frames
    per = height // tm
    cells = frames * columns
    part = channels // tm
    share = part // 2
    width = share // pairs
    full = 3 * part
    segment, z, p = (lax.axis_index(name) for name in AXES)
    core = lax.rem(p, 2)
    y = lax.div(p, 2)

    for own, more, to in ((own_high, more_high, lh), (own_low, more_low, ll)):
        for row in range(per + 4):
            to[z * per + row] = own[z * per + row]
        for i in range(more.shape[0]):
            to[missing_row(z, i, height, per)] = more[i]

    for which in range(2):
        for k in range(tm):
            first = lax.rem(z - k + tm, tm) * per
            ordered = []
            for side in range(2):
                its = core if side == 0 else 1 - core
                for step in range(pairs):
                    its_y = lax.rem(y + step, pairs)
                    start = its * share + its_y * width
                    ordered.append(pieces[k][which, pl.ds(start, width), :])
            x = jnp.concatenate(ordered, axis=0)
            for j in range(per):
                row = x[:, j * cells : (j + 1) * cells]
                column = lax.rem(lax.broadcasted_iota(jnp.int32, row.shape, 1), columns)
                after = jnp.where(column == columns - 1, 0.0, rotate(row, -1, 1))
                before = jnp.where(column == 0, 0.0, rotate(row, 1, 1))
                high, low = split(jnp.concatenate([after, row, before], axis=0))
                field[which, first + j, pl.ds(0, full), :] = high
                field[which, first + j, pl.ds(full, full), :] = low

    for which, (high_ref, low_ref, offset) in enumerate(((xh, xl, 2), (lh, ll, 1))):
        relative = segment if which == 0 else 1 - segment
        left = jnp.concatenate([field[which, row] for row in range(height)], axis=1)
        for a in range(3):
            for b in range(3):
                at = (pl.ds(offset + b, height), pl.ds(a, frames))
                right = jnp.concatenate(
                    [ref[at].reshape(height * cells, channels) for ref in (high_ref, low_ref)], axis=1
                )
                product = dot(left, right)
                total = product[:full, :channels] + product[:full, channels:] + product[full:, :channels]
                for e in range(3):
                    tap = (a * 3 + b) * 3 + e
                    for side, ref in enumerate((keep_ref, send_ref)):
                        for step in range(pairs):
                            start = e * part + side * share + step * width
                            ref[relative, step, tap] = total[start : start + width]


def assembled_kernel(dims, early_ref, late_ref, came_early_ref, came_late_ref, out_ref):
    tm, pairs, channels = dims
    z, p = lax.axis_index("tm"), lax.axis_index("space")
    core = lax.rem(p, 2)
    y = lax.div(p, 2)
    cut = early_ref.shape[2]
    for tap in range(cut + late_ref.shape[2]):
        parts = []
        for target in range(tm):
            k = lax.rem(z - target + tm, tm)
            for side in range(2):
                for its_y in range(pairs):
                    step = lax.rem(y - its_y + pairs, pairs)
                    if tap < cut:
                        kept, came = early_ref[step, k, tap], came_early_ref[step, k, tap]
                    else:
                        kept, came = late_ref[k, step, tap - cut], came_late_ref[k, step, tap - cut]
                    parts.append(jnp.where(core == side, kept, came))
        out_ref[pl.ds(tap * channels, channels), :] = jnp.concatenate(parts, axis=0).T


def vmem(shape, dtype):
    return pltpu.VMEM(shape, dtype)


def call(kernel, shapes, scratch, count, flops, limit, inputs=pltpu.VMEM):
    single = not isinstance(shapes, list)
    space = pl.BlockSpec(memory_space=pltpu.VMEM)
    return pl.pallas_call(
        kernel,
        out_shape=shapes,
        in_specs=[pl.BlockSpec(memory_space=inputs)] * count,
        out_specs=space if single else [space] * len(shapes),
        scratch_shapes=scratch,
        compiler_params=pltpu.CompilerParams(vmem_limit_bytes=limit * MIB),
        cost_estimate=pl.CostEstimate(flops=flops, bytes_accessed=4_000_000, transcendentals=0),
    )


def make_local(sizes):
    segments, tm, space = sizes["segment"], sizes["tm"], sizes["space"]
    pairs = space // 2

    def send(x, move):
        route = []
        for s in range(segments):
            for t in range(tm):
                for p in range(space):
                    target = move(s, t, p)
                    if target is not None:
                        s2, t2, p2 = target
                        route.append(((s * tm + t) * space + p, (s2 * tm + t2) * space + p2))
        return lax.ppermute(x, AXES, route)

    def later(k):
        return lambda s, t, p: (s, (t + k) % tm, p)

    def across(flip, step):
        return lambda s, t, p: (s ^ flip, t, ((p // 2 + step) % pairs) * 2 + p % 2)

    def swap_section(s, t, p):
        return (1 - s, t, p)

    def swap_core(s, t, p):
        return (s, t, p ^ 1)

    def swap_outer(s, t, p):
        target = p - 1 if p % 2 == 0 else p + 1
        return (s, t, target) if 0 <= target < space else None

    def local(video_clips, conv_weights):
        clips, own_frames, height, columns, channels = video_clips.shape
        frames = tm * own_frames
        rows_all = height * space
        per = height // tm
        cells = frames * columns
        factor = float(clips * frames * rows_all * columns) ** (-0.5)
        own = conv_weights[0]
        taps = own.shape[0] // channels
        third = own.shape[0] // 3
        core = lax.axis_index("space") % 2

        early, late, clip = call(
            pick_kernel,
            [
                jax.ShapeDtypeStruct((third, channels), f32),
                jax.ShapeDtypeStruct((third // 2, channels), f32),
                jax.ShapeDtypeStruct(video_clips.shape[1:], f32),
            ],
            [pltpu.SemaphoreType.DMA((3,))],
            2,
            0,
            60,
            pltpu.HBM,
        )(video_clips, conv_weights)
        mine = send(early, swap_section)
        mine_late = send(late, swap_section)
        block = lax.all_gather(clip, "tm")
        bottom, top = block[:, :, height - 3 :], block[:, :, :3]
        to_inner = jnp.where(core == 0, bottom, top)
        to_outer = jnp.where(core == 0, top, bottom)
        inner = send(to_inner, swap_core)
        outer = send(to_outer, swap_outer)
        ready, _, _ = lax.optimization_barrier((mine, to_inner, to_outer))
        other = send(ready, swap_core)
        other_late = send(mine_late, swap_core)

        part = channels // tm
        dims = (tm, own_frames, height, rows_all, columns, channels, factor)
        field = (frames + 2, columns, channels)
        rows = height + 4
        products = 8 * 128 * channels * cells * 9
        shape = jax.ShapeDtypeStruct
        *sent, xh, xl, lh, ll, encoder = call(
            functools.partial(activations_kernel, dims),
            [shape((2, part, per * cells), f32)] * tm
            + [shape((height + 6,) + field, bf16)] * 2
            + [shape((rows,) + field, bf16)] * 2
            + [shape((9 * channels, 6 * channels), bf16)],
            [
                vmem((height + 2, frames, columns, channels), f32),
                vmem((9 * channels, 6 * channels), bf16),
                vmem((9 * channels, 6 * channels), bf16),
                vmem((per + 2,) + field, bf16),
                vmem((per + 2,) + field, bf16),
                vmem((per, frames, columns, channels), f32),
                vmem((2, channels, per * cells), f32),
            ],
            8,
            3 * products * (3 * per + 6),
            32,
        )(block, inner, outer, own, mine, other, mine_late, other_late)

        extra = height - 1 - per
        more_high, more_low = call(
            functools.partial(latents_kernel, dims),
            [shape((extra,) + field, bf16)] * 2,
            [],
            3,
            3 * products * extra,
            12,
        )(xh, xl, encoder)
        pieces = [sent[0]] + [send(sent[k], later(k)) for k in range(1, tm)]
        width = part // (2 * pairs)
        grads = shape((2, pairs, taps, width, channels), f32)
        keep, give = call(
            functools.partial(
                weights_kernel, (tm, own_frames, height, rows_all, columns, channels, pairs)
            ),
            [grads, grads],
            [vmem((2, height, 6 * part, cells), bf16)] + [vmem((rows,) + field, bf16)] * 2,
            tm + 6,
            16 * taps * part * height * cells * channels,
            16,
        )(*pieces, xh, xl, lh, ll, more_high, more_low)

        both = keep + send(give, swap_core)
        total = both[0, 0]
        for flip in range(2):
            for step in range(pairs):
                if flip or step:
                    total = total + send(both[flip, step], across(flip, step))

        cut = taps // 2
        early, late = total[:cut], total[cut:]
        late_rows = [late] + [send(late, across(0, k)) for k in range(1, pairs)]
        early_all = [early] + [send(early, later(k)) for k in range(1, tm)]
        late_rows, early_all = lax.optimization_barrier((late_rows, early_all))
        late_rows, early_all = jnp.stack(late_rows), jnp.stack(early_all)
        early_all = jnp.stack([early_all] + [send(early_all, across(0, k)) for k in range(1, pairs)])
        late_all = jnp.stack([late_rows] + [send(late_rows, later(k)) for k in range(1, tm)])
        came = [send(x, swap_core) for x in (early_all, late_all)]
        out = call(
            functools.partial(assembled_kernel, (tm, pairs, channels)),
            jax.ShapeDtypeStruct(own.shape, f32),
            [],
            4,
            0,
            12,
        )(early_all, late_all, *came)
        return out[None]

    return local


def solution(mesh):
    return jax.shard_map(
        make_local(dict(mesh.shape)),
        mesh=mesh,
        in_specs=(P(None, "tm", "space", None, None), P("segment", None, None)),
        out_specs=P("segment", None, None),
        check_vma=False,
    )
```

```python
import functools

import jax
import jax.numpy as jnp
from jax import lax
from jax.experimental import pallas as pl
from jax.experimental.pallas import tpu as pltpu
from jax.sharding import PartitionSpec as P

f32 = jnp.float32
bf16 = jnp.bfloat16
AXES = ("segment", "tm", "space")
MIB = 1024 * 1024


def split(x):
    high = x.astype(bf16)
    low = (x - high.astype(f32)).astype(bf16)
    return high, low


def dot(a, b):
    return jnp.dot(a, b, preferred_element_type=f32)


def rotate(x, amount, axis):
    size = x.shape[axis]
    amount = amount % size
    if amount == 0:
        return x
    return jnp.concatenate(
        [lax.slice_in_dim(x, size - amount, size, axis=axis), lax.slice_in_dim(x, 0, size - amount, axis=axis)],
        axis=axis,
    )


def store_split(high_ref, low_ref, index, x):
    high, low = split(x)
    high_ref[index] = high
    low_ref[index] = low


def put_taps(to_ref, tap, x):
    channels = x.shape[-1]
    rows = pl.ds((tap // 3) * channels, channels)
    lanes = pl.ds((tap % 3) * channels, channels)
    low_lanes = pl.ds((tap % 3 + 3) * channels, channels)
    high, low = split(x)
    to_ref[rows, lanes] = high
    to_ref[rows, low_lanes] = low
    if tap >= 24:
        rows = pl.ds(9 * channels, channels)
        to_ref[rows, lanes] = high
        to_ref[rows, low_lanes] = jnp.zeros_like(low)


def shifted_sum(y, columns, channels, flip):
    parts = [y[:, i * channels : (i + 1) * channels].reshape(-1, columns, channels) for i in range(3)]
    if flip:
        parts = parts[::-1]
    column = lax.broadcasted_iota(jnp.int32, parts[0].shape, 1)
    first = jnp.where(column == 0, 0.0, rotate(parts[0], 1, 1))
    last = jnp.where(column == columns - 1, 0.0, rotate(parts[2], -1, 1))
    return parts[1] + first + last


def convolved(high_ref, low_ref, places, count, dims, weight_ref, flip=False):
    frames, columns, channels = dims
    high, low = [], []
    for row, a in places:
        at = (pl.ds(row, count), pl.ds(a, frames))
        high.append(high_ref[at].reshape(count * frames * columns, channels))
        low.append(low_ref[at].reshape(count * frames * columns, channels))
    full = 3 * channels
    both = dot(jnp.concatenate(high + low[8:], axis=1), weight_ref[...])
    rest = dot(jnp.concatenate(low[:8], axis=1), weight_ref[pl.ds(0, 8 * channels), pl.ds(0, full)])
    y = both[:, :full] + both[:, full:] + rest
    return shifted_sum(y, columns, channels, flip).reshape(count, frames, columns, channels)


def received_taps(core, refs, tap, channels):
    mine_ref, other_ref, mine_late_ref, other_late_ref = refs
    if tap < 18:
        at = pl.ds((tap % 9) * channels, channels)
        return jnp.where(core == tap // 9, mine_ref[at, :], other_ref[at, :])
    half = mine_late_ref.shape[0]
    start, parts = (tap - 18) * channels, []
    while start < (tap - 17) * channels:
        side = start // half
        stop = min((side + 1) * half, (tap - 17) * channels)
        at = pl.ds(start - side * half, stop - start)
        parts.append(jnp.where(core == side, mine_late_ref[at, :], other_late_ref[at, :]))
        start = stop
    return parts[0] if len(parts) == 1 else jnp.concatenate(parts, axis=0)


def field_rows(high_ref, low_ref, row, shape, weight_ref):
    places = [(row + b, a) for a in range(3) for b in range(3)]
    return convolved(high_ref, low_ref, places, 1, shape, weight_ref)[0]


def store_latent(high_ref, low_ref, row, place, rows_all, value):
    latent = value / (1.0 + jnp.exp(-value))
    inside = jnp.logical_and(place >= 0, place < rows_all)
    frames = value.shape[0]
    store_split(high_ref, low_ref, (row, pl.ds(2, frames)), jnp.where(inside, latent, 0.0))


def missing_row(z, i, height, per):
    below = jnp.maximum(z * per - 1, 0)
    row = jnp.where(i < below, 1 + i, z * per + per + 4 + i - below)
    return jnp.minimum(row, height + 3)


def latents_kernel(dims, xh, xl, encoder, lh, ll):
    tm, own_frames, height, rows_all, columns, channels, factor = dims
    frames = tm * own_frames
    per = height // tm
    z, p = lax.axis_index("tm"), lax.axis_index("space")
    for ref in (lh, ll):
        ref[:, 0:2] = jnp.zeros((ref.shape[0], 2) + ref.shape[2:], bf16)
    for i in range(lh.shape[0]):
        row = missing_row(z, i, height, per)
        value = field_rows(xh, xl, row, (frames, columns, channels), encoder)
        store_latent(lh, ll, i, p * height + row - 2, rows_all, value)


def pick_kernel(video_ref, weights_ref, early_ref, late_ref, clip_ref, sems):
    early, late = early_ref.shape[0], late_ref.shape[0]
    segment, core = lax.axis_index("segment"), lax.rem(lax.axis_index("space"), 2)
    copies = [
        pltpu.make_async_copy(weights_ref.at[0, pl.ds(core * early, early)], early_ref, sems.at[0]),
        pltpu.make_async_copy(weights_ref.at[0, pl.ds(2 * early + core * late, late)], late_ref, sems.at[1]),
        pltpu.make_async_copy(video_ref.at[segment], clip_ref, sems.at[2]),
    ]
    for copy in copies:
        copy.start()
    for copy in copies:
        copy.wait()


def activations_kernel(
    dims, block_ref, inner_ref, outer_ref, own_ref, *refs
):
    tm, own_frames, height, rows_all, columns, channels, factor = dims
    came_refs, sent_refs = refs[:4], refs[4 : 4 + tm]
    xh, xl, lh, ll, encoder, video, decoder, turned, ch, cl, hidden, grads = refs[4 + tm :]
    frames = tm * own_frames
    per = height // tm
    cells = frames * columns
    shape = (frames, columns, channels)
    segment, z, p = (lax.axis_index(name) for name in AXES)
    core = lax.rem(p, 2)

    for tap in range(27):
        own = own_ref[pl.ds(tap * channels, channels), :]
        came = received_taps(core, came_refs, tap, channels)
        put_taps(encoder, tap, jnp.where(segment == 0, own, came))
        block = jnp.where(segment == 0, came, own)
        put_taps(decoder, tap, block)
        put_taps(turned, tap, block.T)
    for ref in (xh, xl, lh, ll):
        ref[:, 0:2] = jnp.zeros((ref.shape[0], 2) + ref.shape[2:], bf16)
    for ref in (ch, cl):
        ref[:, frames:] = jnp.zeros((ref.shape[0], 2) + ref.shape[2:], bf16)

    for k in range(tm):
        first = k * own_frames
        for row in range(-3, height + 3):
            if row < 0:
                x = jnp.where(core == 0, outer_ref[k, :, 3 + row], inner_ref[k, :, 3 + row])
            elif row < height:
                x = block_ref[k, :, row]
            else:
                x = jnp.where(core == 0, inner_ref[k, :, row - height], outer_ref[k, :, row - height])
            store_split(xh, xl, (row + 3, pl.ds(first + 2, own_frames)), x)
            if -1 <= row <= height:
                video[row + 1, pl.ds(first, own_frames)] = x

    start = z * per
    for row in range(per + 4):
        value = field_rows(xh, xl, start + row, shape, encoder)
        if 2 <= row < per + 2:
            hidden[row - 2] = value
        store_latent(lh, ll, start + row, p * height + start + row - 2, rows_all, value)

    for j in range(per + 2):
        row = z * per - 1 + j
        decoded = field_rows(lh, ll, row + 1, shape, decoder)
        place = p * height + row
        inside = jnp.logical_and(place >= 0, place < rows_all)
        cotangent = jnp.where(inside, (decoded - video[row + 1]) * factor, 0.0)
        store_split(ch, cl, (j, pl.ds(0, frames)), cotangent)
        if 1 <= j <= per:
            grads[1, :, pl.ds((j - 1) * cells, cells)] = cotangent.reshape(cells, channels).T

    for j in range(per):
        places = [(j + 2 - b, 2 - a) for a in range(3) for b in range(3)]
        grad_latent = convolved(ch, cl, places, 1, shape, turned, flip=True)[0]
        value = hidden[j]
        sigmoid = 1.0 / (1.0 + jnp.exp(-value))
        grad = grad_latent * (sigmoid * (1.0 + value * (1.0 - sigmoid)))
        grads[0, :, pl.ds(j * cells, cells)] = grad.reshape(cells, channels).T

    part = channels // tm
    for k, ref in enumerate(sent_refs):
        target = lax.rem(z + k, tm)
        at = pl.ds(pl.multiple_of(target * part, part), part)
        for which in range(2):
            ref[which] = grads[which, at, :]


def weights_kernel(dims, *refs):
    tm, own_frames, height, rows_all, columns, channels, pairs = dims
    pieces = refs[:tm]
    xh, xl, own_high, own_low, more_high, more_low, keep_ref, send_ref, field, lh, ll = refs[tm:]
    frames = tm * own_frames
    per = height // tm
    cells = frames * columns
    part = channels // tm
    share = part // 2
    width = share // pairs
    full = 3 * part
    segment, z, p = (lax.axis_index(name) for name in AXES)
    core = lax.rem(p, 2)
    y = lax.div(p, 2)

    for own, more, to in ((own_high, more_high, lh), (own_low, more_low, ll)):
        for row in range(per + 4):
            to[z * per + row] = own[z * per + row]
        for i in range(more.shape[0]):
            to[missing_row(z, i, height, per)] = more[i]

    for which in range(2):
        for k in range(tm):
            first = lax.rem(z - k + tm, tm) * per
            ordered = []
            for side in range(2):
                its = core if side == 0 else 1 - core
                for step in range(pairs):
                    its_y = lax.rem(y + step, pairs)
                    start = its * share + its_y * width
                    ordered.append(pieces[k][which, pl.ds(start, width), :])
            x = jnp.concatenate(ordered, axis=0)
            for j in range(per):
                row = x[:, j * cells : (j + 1) * cells]
                column = lax.rem(lax.broadcasted_iota(jnp.int32, row.shape, 1), columns)
                after = jnp.where(column == columns - 1, 0.0, rotate(row, -1, 1))
                before = jnp.where(column == 0, 0.0, rotate(row, 1, 1))
                high, low = split(jnp.concatenate([after, row, before], axis=0))
                field[which, first + j, pl.ds(0, full), :] = high
                field[which, first + j, pl.ds(full, full), :] = low

    for which, (high_ref, low_ref, offset) in enumerate(((xh, xl, 2), (lh, ll, 1))):
        relative = segment if which == 0 else 1 - segment
        left = jnp.concatenate([field[which, row] for row in range(height)], axis=1)
        for a in range(3):
            for b in range(3):
                at = (pl.ds(offset + b, height), pl.ds(a, frames))
                right = jnp.concatenate(
                    [ref[at].reshape(height * cells, channels) for ref in (high_ref, low_ref)], axis=1
                )
                product = dot(left, right)
                total = product[:full, :channels] + product[:full, channels:] + product[full:, :channels]
                for e in range(3):
                    tap = (a * 3 + b) * 3 + e
                    for side, ref in enumerate((keep_ref, send_ref)):
                        for step in range(pairs):
                            start = e * part + side * share + step * width
                            ref[relative, step, tap] = total[start : start + width]


def assembled_kernel(dims, early_ref, late_ref, came_early_ref, came_late_ref, out_ref):
    tm, pairs, channels = dims
    z, p = lax.axis_index("tm"), lax.axis_index("space")
    core = lax.rem(p, 2)
    y = lax.div(p, 2)
    cut = early_ref.shape[2]
    for tap in range(cut + late_ref.shape[2]):
        parts = []
        for target in range(tm):
            k = lax.rem(z - target + tm, tm)
            for side in range(2):
                for its_y in range(pairs):
                    step = lax.rem(y - its_y + pairs, pairs)
                    if tap < cut:
                        kept, came = early_ref[step, k, tap], came_early_ref[step, k, tap]
                    else:
                        kept, came = late_ref[k, step, tap - cut], came_late_ref[k, step, tap - cut]
                    parts.append(jnp.where(core == side, kept, came))
        out_ref[pl.ds(tap * channels, channels), :] = jnp.concatenate(parts, axis=0).T


def vmem(shape, dtype):
    return pltpu.VMEM(shape, dtype)


def call(kernel, shapes, scratch, count, flops, limit, inputs=pltpu.VMEM):
    single = not isinstance(shapes, list)
    space = pl.BlockSpec(memory_space=pltpu.VMEM)
    return pl.pallas_call(
        kernel,
        out_shape=shapes,
        in_specs=[pl.BlockSpec(memory_space=inputs)] * count,
        out_specs=space if single else [space] * len(shapes),
        scratch_shapes=scratch,
        compiler_params=pltpu.CompilerParams(vmem_limit_bytes=limit * MIB),
        cost_estimate=pl.CostEstimate(flops=flops, bytes_accessed=4_000_000, transcendentals=0),
    )


def make_local(sizes):
    segments, tm, space = sizes["segment"], sizes["tm"], sizes["space"]
    pairs = space // 2

    def send(x, move):
        route = []
        for s in range(segments):
            for t in range(tm):
                for p in range(space):
                    target = move(s, t, p)
                    if target is not None:
                        s2, t2, p2 = target
                        route.append(((s * tm + t) * space + p, (s2 * tm + t2) * space + p2))
        return lax.ppermute(x, AXES, route)

    def later(k):
        return lambda s, t, p: (s, (t + k) % tm, p)

    def across(flip, step):
        return lambda s, t, p: (s ^ flip, t, ((p // 2 + step) % pairs) * 2 + p % 2)

    def swap_section(s, t, p):
        return (1 - s, t, p)

    def swap_core(s, t, p):
        return (s, t, p ^ 1)

    def swap_outer(s, t, p):
        target = p - 1 if p % 2 == 0 else p + 1
        return (s, t, target) if 0 <= target < space else None

    def local(video_clips, conv_weights):
        clips, own_frames, height, columns, channels = video_clips.shape
        frames = tm * own_frames
        rows_all = height * space
        per = height // tm
        cells = frames * columns
        factor = float(clips * frames * rows_all * columns) ** (-0.5)
        own = conv_weights[0]
        taps = own.shape[0] // channels
        third = own.shape[0] // 3
        core = lax.axis_index("space") % 2

        early, late, clip = call(
            pick_kernel,
            [
                jax.ShapeDtypeStruct((third, channels), f32),
                jax.ShapeDtypeStruct((third // 2, channels), f32),
                jax.ShapeDtypeStruct(video_clips.shape[1:], f32),
            ],
            [pltpu.SemaphoreType.DMA((3,))],
            2,
            0,
            60,
            pltpu.HBM,
        )(video_clips, conv_weights)
        mine = send(early, swap_section)
        mine_late = send(late, swap_section)
        block = lax.all_gather(clip, "tm")
        bottom, top = block[:, :, height - 3 :], block[:, :, :3]
        to_inner = jnp.where(core == 0, bottom, top)
        to_outer = jnp.where(core == 0, top, bottom)
        inner = send(to_inner, swap_core)
        outer = send(to_outer, swap_outer)
        ready, _, _ = lax.optimization_barrier((mine, to_inner, to_outer))
        other = send(ready, swap_core)
        other_late = send(mine_late, swap_core)

        part = channels // tm
        dims = (tm, own_frames, height, rows_all, columns, channels, factor)
        field = (frames + 2, columns, channels)
        rows = height + 4
        products = 8 * 128 * channels * cells * 9
        shape = jax.ShapeDtypeStruct
        *sent, xh, xl, lh, ll, encoder = call(
            functools.partial(activations_kernel, dims),
            [shape((2, part, per * cells), f32)] * tm
            + [shape((height + 6,) + field, bf16)] * 2
            + [shape((rows,) + field, bf16)] * 2
            + [shape((10 * channels, 6 * channels), bf16)],
            [
                vmem((height + 2, frames, columns, channels), f32),
                vmem((10 * channels, 6 * channels), bf16),
                vmem((10 * channels, 6 * channels), bf16),
                vmem((per + 2,) + field, bf16),
                vmem((per + 2,) + field, bf16),
                vmem((per, frames, columns, channels), f32),
                vmem((2, channels, per * cells), f32),
            ],
            8,
            3 * products * (3 * per + 6),
            32,
        )(block, inner, outer, own, mine, other, mine_late, other_late)

        extra = height - 1 - per
        more_high, more_low = call(
            functools.partial(latents_kernel, dims),
            [shape((extra,) + field, bf16)] * 2,
            [],
            3,
            3 * products * extra,
            12,
        )(xh, xl, encoder)
        pieces = [sent[0]] + [send(sent[k], later(k)) for k in range(1, tm)]
        width = part // (2 * pairs)
        grads = shape((2, pairs, taps, width, channels), f32)
        keep, give = call(
            functools.partial(
                weights_kernel, (tm, own_frames, height, rows_all, columns, channels, pairs)
            ),
            [grads, grads],
            [vmem((2, height, 6 * part, cells), bf16)] + [vmem((rows,) + field, bf16)] * 2,
            tm + 6,
            16 * taps * part * height * cells * channels,
            16,
        )(*pieces, xh, xl, lh, ll, more_high, more_low)

        both = keep + send(give, swap_core)
        total = both[0, 0]
        for flip in range(2):
            for step in range(pairs):
                if flip or step:
                    total = total + send(both[flip, step], across(flip, step))

        cut = 2 * taps // 3
        early, late = total[:cut], total[cut:]
        late_rows = [late] + [send(late, across(0, k)) for k in range(1, pairs)]
        early_all = [early] + [send(early, later(k)) for k in range(1, tm)]
        late_rows, early_all = lax.optimization_barrier((late_rows, early_all))
        late_rows, early_all = jnp.stack(late_rows), jnp.stack(early_all)
        early_all = jnp.stack([early_all] + [send(early_all, across(0, k)) for k in range(1, pairs)])
        late_all = jnp.stack([late_rows] + [send(late_rows, later(k)) for k in range(1, tm)])
        early_all, late_all = lax.optimization_barrier((early_all, late_all))
        came = [send(x, swap_core) for x in (early_all, late_all)]
        out = call(
            functools.partial(assembled_kernel, (tm, pairs, channels)),
            jax.ShapeDtypeStruct(own.shape, f32),
            [],
            4,
            0,
            12,
        )(early_all, late_all, *came)
        return out[None]

    return local


def solution(mesh):
    return jax.shard_map(
        make_local(dict(mesh.shape)),
        mesh=mesh,
        in_specs=(P(None, "tm", "space", None, None), P("segment", None, None)),
        out_specs=P("segment", None, None),
        check_vma=False,
    )
```

```python
import functools

import jax
import jax.numpy as jnp
from jax import lax
from jax.experimental import pallas as pl
from jax.experimental.pallas import tpu as pltpu
from jax.sharding import PartitionSpec as P

f32 = jnp.float32
bf16 = jnp.bfloat16
AXES = ("segment", "tm", "space")
MIB = 1024 * 1024


def split(x):
    high = x.astype(bf16)
    low = (x - high.astype(f32)).astype(bf16)
    return high, low


def dot(a, b):
    return jnp.dot(a, b, preferred_element_type=f32)


def rotate(x, amount, axis):
    size = x.shape[axis]
    amount = amount % size
    if amount == 0:
        return x
    return jnp.concatenate(
        [lax.slice_in_dim(x, size - amount, size, axis=axis), lax.slice_in_dim(x, 0, size - amount, axis=axis)],
        axis=axis,
    )


def store_split(high_ref, low_ref, index, x):
    high, low = split(x)
    high_ref[index] = high
    low_ref[index] = low


def put_taps(to_ref, tap, x):
    channels = x.shape[-1]
    rows = pl.ds((tap // 3) * channels, channels)
    lanes = pl.ds((tap % 3) * channels, channels)
    low_lanes = pl.ds((tap % 3 + 3) * channels, channels)
    high, low = split(x)
    to_ref[rows, lanes] = high
    to_ref[rows, low_lanes] = low
    if tap >= 24:
        rows = pl.ds(9 * channels, channels)
        to_ref[rows, lanes] = high
        to_ref[rows, low_lanes] = jnp.zeros_like(low)


def shifted_sum(y, columns, channels, flip):
    parts = [y[:, i * channels : (i + 1) * channels].reshape(-1, columns, channels) for i in range(3)]
    if flip:
        parts = parts[::-1]
    column = lax.broadcasted_iota(jnp.int32, parts[0].shape, 1)
    first = jnp.where(column == 0, 0.0, rotate(parts[0], 1, 1))
    last = jnp.where(column == columns - 1, 0.0, rotate(parts[2], -1, 1))
    return parts[1] + first + last


def convolved(high_ref, low_ref, places, count, dims, weight_ref, flip=False):
    frames, columns, channels = dims
    high, low = [], []
    for row, a in places:
        at = (pl.ds(row, count), pl.ds(a, frames))
        high.append(high_ref[at].reshape(count * frames * columns, channels))
        low.append(low_ref[at].reshape(count * frames * columns, channels))
    full = 3 * channels
    both = dot(jnp.concatenate(high + low[8:], axis=1), weight_ref[...])
    rest = dot(jnp.concatenate(low[:8], axis=1), weight_ref[pl.ds(0, 8 * channels), pl.ds(0, full)])
    y = both[:, :full] + both[:, full:] + rest
    return shifted_sum(y, columns, channels, flip).reshape(count, frames, columns, channels)


def received_taps(core, refs, tap, channels):
    mine_ref, other_ref, mine_late_ref, other_late_ref = refs
    if tap < 18:
        at = pl.ds((tap % 9) * channels, channels)
        return jnp.where(core == tap // 9, mine_ref[at, :], other_ref[at, :])
    half = mine_late_ref.shape[0]
    start, parts = (tap - 18) * channels, []
    while start < (tap - 17) * channels:
        side = start // half
        stop = min((side + 1) * half, (tap - 17) * channels)
        at = pl.ds(start - side * half, stop - start)
        parts.append(jnp.where(core == side, mine_late_ref[at, :], other_late_ref[at, :]))
        start = stop
    return parts[0] if len(parts) == 1 else jnp.concatenate(parts, axis=0)


def field_rows(high_ref, low_ref, row, shape, weight_ref):
    places = [(row + b, a) for a in range(3) for b in range(3)]
    return convolved(high_ref, low_ref, places, 1, shape, weight_ref)[0]


def store_latent(high_ref, low_ref, row, place, rows_all, value):
    latent = value / (1.0 + jnp.exp(-value))
    inside = jnp.logical_and(place >= 0, place < rows_all)
    frames = value.shape[0]
    store_split(high_ref, low_ref, (row, pl.ds(2, frames)), jnp.where(inside, latent, 0.0))


def missing_row(z, i, height, per):
    below = jnp.maximum(z * per - 1, 0)
    row = jnp.where(i < below, 1 + i, z * per + per + 4 + i - below)
    return jnp.minimum(row, height + 3)


def latents_kernel(dims, xh, xl, encoder, lh, ll):
    tm, own_frames, height, rows_all, columns, channels, factor = dims
    frames = tm * own_frames
    per = height // tm
    z, p = lax.axis_index("tm"), lax.axis_index("space")
    for ref in (lh, ll):
        ref[:, 0:2] = jnp.zeros((ref.shape[0], 2) + ref.shape[2:], bf16)
    for i in range(lh.shape[0]):
        row = missing_row(z, i, height, per)
        value = field_rows(xh, xl, row, (frames, columns, channels), encoder)
        store_latent(lh, ll, i, p * height + row - 2, rows_all, value)


def pick_kernel(video_ref, weights_ref, early_ref, late_ref, clip_ref, sems):
    early, late = early_ref.shape[0], late_ref.shape[0]
    segment, core = lax.axis_index("segment"), lax.rem(lax.axis_index("space"), 2)
    copies = [
        pltpu.make_async_copy(weights_ref.at[0, pl.ds(core * early, early)], early_ref, sems.at[0]),
        pltpu.make_async_copy(weights_ref.at[0, pl.ds(2 * early + core * late, late)], late_ref, sems.at[1]),
        pltpu.make_async_copy(video_ref.at[segment], clip_ref, sems.at[2]),
    ]
    for copy in copies:
        copy.start()
    for copy in copies:
        copy.wait()


def first_rows(z, height, per):
    return jnp.clip(z * per, 1, height - 3)


def first_kernel(dims, block_ref, own_ref, *refs):
    tm, own_frames, height, rows_all, columns, channels, factor = dims
    came_refs, (encoder, decoder, turned, begun_high, begun_low, begun, xh, xl) = refs[:4], refs[4:]
    frames = tm * own_frames
    per = height // tm
    segment, z, p = (lax.axis_index(name) for name in AXES)
    core = lax.rem(p, 2)

    for tap in range(27):
        own = own_ref[pl.ds(tap * channels, channels), :]
        came = received_taps(core, came_refs, tap, channels)
        put_taps(encoder, tap, jnp.where(segment == 0, own, came))
        block = jnp.where(segment == 0, came, own)
        put_taps(decoder, tap, block)
        put_taps(turned, tap, block.T)
    for ref in (xh, xl, begun_high, begun_low):
        ref[:, 0:2] = jnp.zeros((ref.shape[0], 2) + ref.shape[2:], bf16)
    for k in range(tm):
        for row in range(height):
            at = (row, pl.ds(k * own_frames + 2, own_frames))
            store_split(xh, xl, at, block_ref[k, :, row])
    row = first_rows(z, height, per)
    for i in range(2):
        value = field_rows(xh, xl, row + i - 1, (frames, columns, channels), encoder)
        begun[i] = value
        store_latent(begun_high, begun_low, i, p * height + row + i, rows_all, value)


def activations_kernel(
    dims, block_ref, inner_ref, outer_ref, encoder, decoder, turned, begun_high, begun_low, begun, *refs
):
    tm, own_frames, height, rows_all, columns, channels, factor = dims
    sent_refs = refs[:tm]
    xh, xl, lh, ll, video, ch, cl, hidden, grads = refs[tm:]
    frames = tm * own_frames
    per = height // tm
    cells = frames * columns
    shape = (frames, columns, channels)
    segment, z, p = (lax.axis_index(name) for name in AXES)
    core = lax.rem(p, 2)

    for ref in (xh, xl, lh, ll):
        ref[:, 0:2] = jnp.zeros((ref.shape[0], 2) + ref.shape[2:], bf16)
    for ref in (ch, cl):
        ref[:, frames:] = jnp.zeros((ref.shape[0], 2) + ref.shape[2:], bf16)

    for k in range(tm):
        first = k * own_frames
        for row in range(-3, height + 3):
            if row < 0:
                x = jnp.where(core == 0, outer_ref[k, :, 3 + row], inner_ref[k, :, 3 + row])
            elif row < height:
                x = block_ref[k, :, row]
            else:
                x = jnp.where(core == 0, inner_ref[k, :, row - height], outer_ref[k, :, row - height])
            store_split(xh, xl, (row + 3, pl.ds(first + 2, own_frames)), x)
            if -1 <= row <= height:
                video[row + 1, pl.ds(first, own_frames)] = x

    start = z * per
    row_begun = first_rows(z, height, per)
    skip = row_begun + 2 - start
    for i in range(2):
        lh[row_begun + 2 + i] = begun_high[i]
        ll[row_begun + 2 + i] = begun_low[i]
        hidden[skip + i] = begun[i]
    for i in range(per + 2):
        row = i + jnp.where(i >= skip, 2, 0)
        value = field_rows(xh, xl, start + row, shape, encoder)
        hidden[row] = value
        store_latent(lh, ll, start + row, p * height + start + row - 2, rows_all, value)

    for j in range(per + 2):
        row = z * per - 1 + j
        decoded = field_rows(lh, ll, row + 1, shape, decoder)
        place = p * height + row
        inside = jnp.logical_and(place >= 0, place < rows_all)
        cotangent = jnp.where(inside, (decoded - video[row + 1]) * factor, 0.0)
        store_split(ch, cl, (j, pl.ds(0, frames)), cotangent)
        if 1 <= j <= per:
            grads[1, :, pl.ds((j - 1) * cells, cells)] = cotangent.reshape(cells, channels).T

    for j in range(per):
        places = [(j + 2 - b, 2 - a) for a in range(3) for b in range(3)]
        grad_latent = convolved(ch, cl, places, 1, shape, turned, flip=True)[0]
        value = hidden[j + 2]
        sigmoid = 1.0 / (1.0 + jnp.exp(-value))
        grad = grad_latent * (sigmoid * (1.0 + value * (1.0 - sigmoid)))
        grads[0, :, pl.ds(j * cells, cells)] = grad.reshape(cells, channels).T

    part = channels // tm
    for k, ref in enumerate(sent_refs):
        target = lax.rem(z + k, tm)
        at = pl.ds(pl.multiple_of(target * part, part), part)
        for which in range(2):
            ref[which] = grads[which, at, :]


def weights_kernel(dims, *refs):
    tm, own_frames, height, rows_all, columns, channels, pairs = dims
    pieces = refs[:tm]
    xh, xl, own_high, own_low, more_high, more_low, keep_ref, send_ref, field, lh, ll = refs[tm:]
    frames = tm * own_frames
    per = height // tm
    cells = frames * columns
    part = channels // tm
    share = part // 2
    width = share // pairs
    full = 3 * part
    segment, z, p = (lax.axis_index(name) for name in AXES)
    core = lax.rem(p, 2)
    y = lax.div(p, 2)

    for own, more, to in ((own_high, more_high, lh), (own_low, more_low, ll)):
        for row in range(per + 4):
            to[z * per + row] = own[z * per + row]
        for i in range(more.shape[0]):
            to[missing_row(z, i, height, per)] = more[i]

    for which in range(2):
        for k in range(tm):
            first = lax.rem(z - k + tm, tm) * per
            ordered = []
            for side in range(2):
                its = core if side == 0 else 1 - core
                for step in range(pairs):
                    its_y = lax.rem(y + step, pairs)
                    start = its * share + its_y * width
                    ordered.append(pieces[k][which, pl.ds(start, width), :])
            x = jnp.concatenate(ordered, axis=0)
            for j in range(per):
                row = x[:, j * cells : (j + 1) * cells]
                column = lax.rem(lax.broadcasted_iota(jnp.int32, row.shape, 1), columns)
                after = jnp.where(column == columns - 1, 0.0, rotate(row, -1, 1))
                before = jnp.where(column == 0, 0.0, rotate(row, 1, 1))
                high, low = split(jnp.concatenate([after, row, before], axis=0))
                field[which, first + j, pl.ds(0, full), :] = high
                field[which, first + j, pl.ds(full, full), :] = low

    for which, (high_ref, low_ref, offset) in enumerate(((xh, xl, 2), (lh, ll, 1))):
        relative = segment if which == 0 else 1 - segment
        left = jnp.concatenate([field[which, row] for row in range(height)], axis=1)
        for a in range(3):
            for b in range(3):
                at = (pl.ds(offset + b, height), pl.ds(a, frames))
                right = jnp.concatenate(
                    [ref[at].reshape(height * cells, channels) for ref in (high_ref, low_ref)], axis=1
                )
                product = dot(left, right)
                total = product[:full, :channels] + product[:full, channels:] + product[full:, :channels]
                for e in range(3):
                    tap = (a * 3 + b) * 3 + e
                    for side, ref in enumerate((keep_ref, send_ref)):
                        for step in range(pairs):
                            start = e * part + side * share + step * width
                            ref[relative, step, tap] = total[start : start + width]


def assembled_kernel(dims, early_ref, late_ref, came_early_ref, came_late_ref, out_ref):
    tm, pairs, channels = dims
    z, p = lax.axis_index("tm"), lax.axis_index("space")
    core = lax.rem(p, 2)
    y = lax.div(p, 2)
    cut = early_ref.shape[2]
    for tap in range(cut + late_ref.shape[2]):
        parts = []
        for target in range(tm):
            k = lax.rem(z - target + tm, tm)
            for side in range(2):
                for its_y in range(pairs):
                    step = lax.rem(y - its_y + pairs, pairs)
                    if tap < cut:
                        kept, came = early_ref[step, k, tap], came_early_ref[step, k, tap]
                    else:
                        kept, came = late_ref[k, step, tap - cut], came_late_ref[k, step, tap - cut]
                    parts.append(jnp.where(core == side, kept, came))
        out_ref[pl.ds(tap * channels, channels), :] = jnp.concatenate(parts, axis=0).T


def vmem(shape, dtype):
    return pltpu.VMEM(shape, dtype)


def call(kernel, shapes, scratch, count, flops, limit, inputs=pltpu.VMEM):
    single = not isinstance(shapes, list)
    space = pl.BlockSpec(memory_space=pltpu.VMEM)
    return pl.pallas_call(
        kernel,
        out_shape=shapes,
        in_specs=[pl.BlockSpec(memory_space=inputs)] * count,
        out_specs=space if single else [space] * len(shapes),
        scratch_shapes=scratch,
        compiler_params=pltpu.CompilerParams(vmem_limit_bytes=limit * MIB),
        cost_estimate=pl.CostEstimate(flops=flops, bytes_accessed=4_000_000, transcendentals=0),
    )


def make_local(sizes):
    segments, tm, space = sizes["segment"], sizes["tm"], sizes["space"]
    pairs = space // 2

    def send(x, move):
        route = []
        for s in range(segments):
            for t in range(tm):
                for p in range(space):
                    target = move(s, t, p)
                    if target is not None:
                        s2, t2, p2 = target
                        route.append(((s * tm + t) * space + p, (s2 * tm + t2) * space + p2))
        return lax.ppermute(x, AXES, route)

    def later(k):
        return lambda s, t, p: (s, (t + k) % tm, p)

    def across(flip, step):
        return lambda s, t, p: (s ^ flip, t, ((p // 2 + step) % pairs) * 2 + p % 2)

    def swap_section(s, t, p):
        return (1 - s, t, p)

    def swap_core(s, t, p):
        return (s, t, p ^ 1)

    def swap_outer(s, t, p):
        target = p - 1 if p % 2 == 0 else p + 1
        return (s, t, target) if 0 <= target < space else None

    def local(video_clips, conv_weights):
        clips, own_frames, height, columns, channels = video_clips.shape
        frames = tm * own_frames
        rows_all = height * space
        per = height // tm
        cells = frames * columns
        factor = float(clips * frames * rows_all * columns) ** (-0.5)
        own = conv_weights[0]
        taps = own.shape[0] // channels
        third = own.shape[0] // 3
        core = lax.axis_index("space") % 2

        early, late, clip = call(
            pick_kernel,
            [
                jax.ShapeDtypeStruct((third, channels), f32),
                jax.ShapeDtypeStruct((third // 2, channels), f32),
                jax.ShapeDtypeStruct(video_clips.shape[1:], f32),
            ],
            [pltpu.SemaphoreType.DMA((3,))],
            2,
            0,
            60,
            pltpu.HBM,
        )(video_clips, conv_weights)
        mine = send(early, swap_section)
        mine_late = send(late, swap_section)
        block = lax.all_gather(clip, "tm")
        bottom, top = block[:, :, height - 3 :], block[:, :, :3]
        to_inner = jnp.where(core == 0, bottom, top)
        to_outer = jnp.where(core == 0, top, bottom)
        inner = send(to_inner, swap_core)
        outer = send(to_outer, swap_outer)
        ready, _, _ = lax.optimization_barrier((mine, to_inner, to_outer))
        other = send(ready, swap_core)
        other_late = send(mine_late, swap_core)

        part = channels // tm
        dims = (tm, own_frames, height, rows_all, columns, channels, factor)
        field = (frames + 2, columns, channels)
        rows = height + 4
        products = 8 * 128 * channels * cells * 9
        shape = jax.ShapeDtypeStruct
        taken = shape((10 * channels, 6 * channels), bf16)
        encoder, decoder, turned, *begun = call(
            functools.partial(first_kernel, dims),
            [taken] * 3 + [shape((2,) + field, bf16)] * 2 + [shape((2, frames, columns, channels), f32)],
            [vmem((height,) + field, bf16)] * 2,
            6,
            0,
            24,
        )(block, own, mine, other, mine_late, other_late)

        *sent, xh, xl, lh, ll = call(
            functools.partial(activations_kernel, dims),
            [shape((2, part, per * cells), f32)] * tm
            + [shape((height + 6,) + field, bf16)] * 2
            + [shape((rows,) + field, bf16)] * 2,
            [
                vmem((height + 2, frames, columns, channels), f32),
                vmem((per + 2,) + field, bf16),
                vmem((per + 2,) + field, bf16),
                vmem((per + 4, frames, columns, channels), f32),
                vmem((2, channels, per * cells), f32),
            ],
            9,
            3 * products * (3 * per + 4),
            28,
        )(block, inner, outer, encoder, decoder, turned, *begun)

        extra = height - 1 - per
        more_high, more_low = call(
            functools.partial(latents_kernel, dims),
            [shape((extra,) + field, bf16)] * 2,
            [],
            3,
            3 * products * extra,
            12,
        )(xh, xl, encoder)
        pieces = [sent[0]] + [send(sent[k], later(k)) for k in range(1, tm)]
        width = part // (2 * pairs)
        grads = shape((2, pairs, taps, width, channels), f32)
        keep, give = call(
            functools.partial(
                weights_kernel, (tm, own_frames, height, rows_all, columns, channels, pairs)
            ),
            [grads, grads],
            [vmem((2, height, 6 * part, cells), bf16)] + [vmem((rows,) + field, bf16)] * 2,
            tm + 6,
            16 * taps * part * height * cells * channels,
            16,
        )(*pieces, xh, xl, lh, ll, more_high, more_low)

        both = keep + send(give, swap_core)
        total = both[0, 0]
        for flip in range(2):
            for step in range(pairs):
                if flip or step:
                    total = total + send(both[flip, step], across(flip, step))

        cut = 2 * taps // 3
        early, late = total[:cut], total[cut:]
        late_rows = [late] + [send(late, across(0, k)) for k in range(1, pairs)]
        early_all = [early] + [send(early, later(k)) for k in range(1, tm)]
        late_rows, early_all = lax.optimization_barrier((late_rows, early_all))
        late_rows, early_all = jnp.stack(late_rows), jnp.stack(early_all)
        early_all = jnp.stack([early_all] + [send(early_all, across(0, k)) for k in range(1, pairs)])
        late_all = jnp.stack([late_rows] + [send(late_rows, later(k)) for k in range(1, tm)])
        early_all, late_all = lax.optimization_barrier((early_all, late_all))
        came = [send(x, swap_core) for x in (early_all, late_all)]
        out = call(
            functools.partial(assembled_kernel, (tm, pairs, channels)),
            jax.ShapeDtypeStruct(own.shape, f32),
            [],
            4,
            0,
            12,
        )(early_all, late_all, *came)
        return out[None]

    return local


def solution(mesh):
    return jax.shard_map(
        make_local(dict(mesh.shape)),
        mesh=mesh,
        in_specs=(P(None, "tm", "space", None, None), P("segment", None, None)),
        out_specs=P("segment", None, None),
        check_vma=False,
    )
```

```python
import functools

import jax
import jax.numpy as jnp
from jax import lax
from jax.experimental import pallas as pl
from jax.experimental.pallas import tpu as pltpu
from jax.sharding import PartitionSpec as P

f32 = jnp.float32
bf16 = jnp.bfloat16
AXES = ("segment", "tm", "space")
MIB = 1024 * 1024


def split(x):
    high = x.astype(bf16)
    low = (x - high.astype(f32)).astype(bf16)
    return high, low


def dot(a, b):
    return jnp.dot(a, b, preferred_element_type=f32)


def rotate(x, amount, axis):
    size = x.shape[axis]
    amount = amount % size
    if amount == 0:
        return x
    return jnp.concatenate(
        [lax.slice_in_dim(x, size - amount, size, axis=axis), lax.slice_in_dim(x, 0, size - amount, axis=axis)],
        axis=axis,
    )


def store_split(high_ref, low_ref, index, x):
    high, low = split(x)
    high_ref[index] = high
    low_ref[index] = low


def put_taps(to_ref, tap, x):
    channels = x.shape[-1]
    rows = pl.ds((tap // 3) * channels, channels)
    lanes = pl.ds((tap % 3) * channels, channels)
    low_lanes = pl.ds((tap % 3 + 3) * channels, channels)
    high, low = split(x)
    to_ref[rows, lanes] = high
    to_ref[rows, low_lanes] = low
    if tap >= 24:
        rows = pl.ds(9 * channels, channels)
        to_ref[rows, lanes] = high
        to_ref[rows, low_lanes] = jnp.zeros_like(low)


def shifted_sum(y, columns, channels, flip):
    parts = [y[:, i * channels : (i + 1) * channels].reshape(-1, columns, channels) for i in range(3)]
    if flip:
        parts = parts[::-1]
    column = lax.broadcasted_iota(jnp.int32, parts[0].shape, 1)
    first = jnp.where(column == 0, 0.0, rotate(parts[0], 1, 1))
    last = jnp.where(column == columns - 1, 0.0, rotate(parts[2], -1, 1))
    return parts[1] + first + last


def convolved(high_ref, low_ref, places, count, dims, weight_ref, flip=False):
    frames, columns, channels = dims
    high, low = [], []
    for row, a in places:
        at = (pl.ds(row, count), pl.ds(a, frames))
        high.append(high_ref[at].reshape(count * frames * columns, channels))
        low.append(low_ref[at].reshape(count * frames * columns, channels))
    full = 3 * channels
    both = dot(jnp.concatenate(high + low[8:], axis=1), weight_ref[...])
    rest = dot(jnp.concatenate(low[:8], axis=1), weight_ref[pl.ds(0, 8 * channels), pl.ds(0, full)])
    y = both[:, :full] + both[:, full:] + rest
    return shifted_sum(y, columns, channels, flip).reshape(count, frames, columns, channels)


def received_taps(core, refs, tap, channels):
    mine_ref, other_ref, mine_late_ref, other_late_ref = refs
    if tap < 18:
        at = pl.ds((tap % 9) * channels, channels)
        return jnp.where(core == tap // 9, mine_ref[at, :], other_ref[at, :])
    half = mine_late_ref.shape[0]
    start, parts = (tap - 18) * channels, []
    while start < (tap - 17) * channels:
        side = start // half
        stop = min((side + 1) * half, (tap - 17) * channels)
        at = pl.ds(start - side * half, stop - start)
        parts.append(jnp.where(core == side, mine_late_ref[at, :], other_late_ref[at, :]))
        start = stop
    return parts[0] if len(parts) == 1 else jnp.concatenate(parts, axis=0)


def field_rows(high_ref, low_ref, row, shape, weight_ref):
    places = [(row + b, a) for a in range(3) for b in range(3)]
    return convolved(high_ref, low_ref, places, 1, shape, weight_ref)[0]


def store_latent(high_ref, low_ref, row, place, rows_all, value):
    latent = value / (1.0 + jnp.exp(-value))
    inside = jnp.logical_and(place >= 0, place < rows_all)
    frames = value.shape[0]
    store_split(high_ref, low_ref, (row, pl.ds(2, frames)), jnp.where(inside, latent, 0.0))


def missing_row(z, i, height, per):
    below = jnp.maximum(z * per - 1, 0)
    row = jnp.where(i < below, 1 + i, z * per + per + 4 + i - below)
    return jnp.minimum(row, height + 3)


def latents_kernel(dims, xh, xl, encoder, lh, ll):
    tm, own_frames, height, rows_all, columns, channels, factor = dims
    frames = tm * own_frames
    per = height // tm
    z, p = lax.axis_index("tm"), lax.axis_index("space")
    for ref in (lh, ll):
        ref[:, 0:2] = jnp.zeros((ref.shape[0], 2) + ref.shape[2:], bf16)
    for i in range(lh.shape[0]):
        row = missing_row(z, i, height, per)
        value = field_rows(xh, xl, row, (frames, columns, channels), encoder)
        store_latent(lh, ll, i, p * height + row - 2, rows_all, value)


def pick_kernel(video_ref, weights_ref, early_ref, late_ref, clip_ref, sems):
    early, late = early_ref.shape[0], late_ref.shape[0]
    segment, core = lax.axis_index("segment"), lax.rem(lax.axis_index("space"), 2)
    copies = [
        pltpu.make_async_copy(weights_ref.at[0, pl.ds(core * early, early)], early_ref, sems.at[0]),
        pltpu.make_async_copy(weights_ref.at[0, pl.ds(2 * early + core * late, late)], late_ref, sems.at[1]),
        pltpu.make_async_copy(video_ref.at[segment], clip_ref, sems.at[2]),
    ]
    for copy in copies:
        copy.start()
    for copy in copies:
        copy.wait()


def first_rows(z, height, per):
    return jnp.clip(z * per, 1, height - 3)


def first_kernel(dims, block_ref, own_ref, *refs):
    tm, own_frames, height, rows_all, columns, channels, factor = dims
    came_refs, (encoder, decoder, turned, begun_high, begun_low, begun, xh, xl) = refs[:4], refs[4:]
    frames = tm * own_frames
    per = height // tm
    segment, z, p = (lax.axis_index(name) for name in AXES)
    core = lax.rem(p, 2)

    for tap in range(27):
        own = own_ref[pl.ds(tap * channels, channels), :]
        came = received_taps(core, came_refs, tap, channels)
        put_taps(encoder, tap, jnp.where(segment == 0, own, came))
        block = jnp.where(segment == 0, came, own)
        put_taps(decoder, tap, block)
        put_taps(turned, tap, block.T)
    for ref in (xh, xl, begun_high, begun_low):
        ref[:, 0:2] = jnp.zeros((ref.shape[0], 2) + ref.shape[2:], bf16)
    for k in range(tm):
        for row in range(height):
            at = (row, pl.ds(k * own_frames + 2, own_frames))
            store_split(xh, xl, at, block_ref[k, :, row])
    row = first_rows(z, height, per)
    for i in range(2):
        value = field_rows(xh, xl, row + i - 1, (frames, columns, channels), encoder)
        begun[i] = value
        store_latent(begun_high, begun_low, i, p * height + row + i, rows_all, value)


def activations_kernel(
    dims, block_ref, inner_ref, outer_ref, encoder, decoder, turned, begun_high, begun_low, begun, *refs
):
    tm, own_frames, height, rows_all, columns, channels, factor = dims
    sent_refs = refs[:tm]
    xh, xl, lh, ll, video, ch, cl, hidden, grads = refs[tm:]
    frames = tm * own_frames
    per = height // tm
    cells = frames * columns
    shape = (frames, columns, channels)
    segment, z, p = (lax.axis_index(name) for name in AXES)
    core = lax.rem(p, 2)

    for ref in (xh, xl, lh, ll):
        ref[:, 0:2] = jnp.zeros((ref.shape[0], 2) + ref.shape[2:], bf16)
    for ref in (ch, cl):
        ref[:, frames:] = jnp.zeros((ref.shape[0], 2) + ref.shape[2:], bf16)

    for k in range(tm):
        first = k * own_frames
        for row in range(-3, height + 3):
            if row < 0:
                x = jnp.where(core == 0, outer_ref[k, :, 3 + row], inner_ref[k, :, 3 + row])
            elif row < height:
                x = block_ref[k, :, row]
            else:
                x = jnp.where(core == 0, inner_ref[k, :, row - height], outer_ref[k, :, row - height])
            store_split(xh, xl, (row + 3, pl.ds(first + 2, own_frames)), x)
            if -1 <= row <= height:
                video[row + 1, pl.ds(first, own_frames)] = x

    start = z * per
    row_begun = first_rows(z, height, per)
    skip = row_begun + 2 - start
    for i in range(2):
        lh[row_begun + 2 + i] = begun_high[i]
        ll[row_begun + 2 + i] = begun_low[i]
        hidden[skip + i] = begun[i]
    for i in range(per + 2):
        row = i + jnp.where(i >= skip, 2, 0)
        value = field_rows(xh, xl, start + row, shape, encoder)
        hidden[row] = value
        store_latent(lh, ll, start + row, p * height + start + row - 2, rows_all, value)

    for j in range(per + 2):
        row = z * per - 1 + j
        decoded = field_rows(lh, ll, row + 1, shape, decoder)
        place = p * height + row
        inside = jnp.logical_and(place >= 0, place < rows_all)
        cotangent = jnp.where(inside, (decoded - video[row + 1]) * factor, 0.0)
        store_split(ch, cl, (j, pl.ds(0, frames)), cotangent)
        if 1 <= j <= per:
            grads[1, :, pl.ds((j - 1) * cells, cells)] = cotangent.reshape(cells, channels).T

    for j in range(per):
        places = [(j + 2 - b, 2 - a) for a in range(3) for b in range(3)]
        grad_latent = convolved(ch, cl, places, 1, shape, turned, flip=True)[0]
        value = hidden[j + 2]
        sigmoid = 1.0 / (1.0 + jnp.exp(-value))
        grad = grad_latent * (sigmoid * (1.0 + value * (1.0 - sigmoid)))
        grads[0, :, pl.ds(j * cells, cells)] = grad.reshape(cells, channels).T

    part = channels // tm
    for k, ref in enumerate(sent_refs):
        target = lax.rem(z + k, tm)
        at = pl.ds(pl.multiple_of(target * part, part), part)
        for which in range(2):
            ref[which] = grads[which, at, :]


def weights_kernel(dims, *refs):
    tm, own_frames, height, rows_all, columns, channels, pairs = dims
    pieces = refs[:tm]
    xh, xl, own_high, own_low, more_high, more_low, keep_ref, send_ref, field, lh, ll = refs[tm:]
    frames = tm * own_frames
    per = height // tm
    cells = frames * columns
    part = channels // tm
    share = part // 2
    width = share // pairs
    full = 3 * part
    segment, z, p = (lax.axis_index(name) for name in AXES)
    core = lax.rem(p, 2)
    y = lax.div(p, 2)

    for own, more, to in ((own_high, more_high, lh), (own_low, more_low, ll)):
        for row in range(per + 4):
            to[z * per + row] = own[z * per + row]
        for i in range(more.shape[0]):
            to[missing_row(z, i, height, per)] = more[i]

    for which in range(2):
        for k in range(tm):
            first = lax.rem(z - k + tm, tm) * per
            ordered = []
            for side in range(2):
                its = core if side == 0 else 1 - core
                for step in range(pairs):
                    its_y = lax.rem(y + step, pairs)
                    start = its * share + its_y * width
                    ordered.append(pieces[k][which, pl.ds(start, width), :])
            x = jnp.concatenate(ordered, axis=0)
            for j in range(per):
                row = x[:, j * cells : (j + 1) * cells]
                column = lax.rem(lax.broadcasted_iota(jnp.int32, row.shape, 1), columns)
                after = jnp.where(column == columns - 1, 0.0, rotate(row, -1, 1))
                before = jnp.where(column == 0, 0.0, rotate(row, 1, 1))
                high, low = split(jnp.concatenate([after, row, before], axis=0))
                field[which, first + j, pl.ds(0, full), :] = high
                field[which, first + j, pl.ds(full, full), :] = low

    for which, (high_ref, low_ref, offset) in enumerate(((xh, xl, 2), (lh, ll, 1))):
        relative = segment if which == 0 else 1 - segment
        left = jnp.concatenate([field[which, row] for row in range(height)], axis=1)
        for a in range(3):
            for b in range(3):
                at = (pl.ds(offset + b, height), pl.ds(a, frames))
                right = jnp.concatenate(
                    [ref[at].reshape(height * cells, channels) for ref in (high_ref, low_ref)], axis=1
                )
                product = dot(left, right)
                total = product[:full, :channels] + product[:full, channels:] + product[full:, :channels]
                for e in range(3):
                    tap = (a * 3 + b) * 3 + e
                    for side, ref in enumerate((keep_ref, send_ref)):
                        for step in range(pairs):
                            start = e * part + side * share + step * width
                            ref[relative, step, tap] = total[start : start + width]


def assembled_kernel(dims, early_ref, late_ref, came_early_ref, came_late_ref, out_ref):
    tm, pairs, channels = dims
    z, p = lax.axis_index("tm"), lax.axis_index("space")
    core = lax.rem(p, 2)
    y = lax.div(p, 2)
    cut = early_ref.shape[2]
    for tap in range(cut + late_ref.shape[2]):
        parts = []
        for target in range(tm):
            k = lax.rem(z - target + tm, tm)
            for side in range(2):
                for its_y in range(pairs):
                    step = lax.rem(y - its_y + pairs, pairs)
                    if tap < cut:
                        kept, came = early_ref[step, k, tap], came_early_ref[step, k, tap]
                    else:
                        kept, came = late_ref[k, step, tap - cut], came_late_ref[k, step, tap - cut]
                    parts.append(jnp.where(core == side, kept, came))
        out_ref[pl.ds(tap * channels, channels), :] = jnp.concatenate(parts, axis=0).T


def vmem(shape, dtype):
    return pltpu.VMEM(shape, dtype)


def call(kernel, shapes, scratch, count, flops, limit, inputs=pltpu.VMEM):
    single = not isinstance(shapes, list)
    space = pl.BlockSpec(memory_space=pltpu.VMEM)
    return pl.pallas_call(
        kernel,
        out_shape=shapes,
        in_specs=[pl.BlockSpec(memory_space=inputs)] * count,
        out_specs=space if single else [space] * len(shapes),
        scratch_shapes=scratch,
        compiler_params=pltpu.CompilerParams(vmem_limit_bytes=limit * MIB),
        cost_estimate=pl.CostEstimate(flops=flops, bytes_accessed=4_000_000, transcendentals=0),
    )


def make_local(sizes):
    segments, tm, space = sizes["segment"], sizes["tm"], sizes["space"]
    pairs = space // 2

    def send(x, move):
        route = []
        for s in range(segments):
            for t in range(tm):
                for p in range(space):
                    target = move(s, t, p)
                    if target is not None:
                        s2, t2, p2 = target
                        route.append(((s * tm + t) * space + p, (s2 * tm + t2) * space + p2))
        return lax.ppermute(x, AXES, route)

    def later(k):
        return lambda s, t, p: (s, (t + k) % tm, p)

    def across(flip, step):
        return lambda s, t, p: (s ^ flip, t, ((p // 2 + step) % pairs) * 2 + p % 2)

    def swap_section(s, t, p):
        return (1 - s, t, p)

    def swap_core(s, t, p):
        return (s, t, p ^ 1)

    def swap_outer(s, t, p):
        target = p - 1 if p % 2 == 0 else p + 1
        return (s, t, target) if 0 <= target < space else None

    def local(video_clips, conv_weights):
        clips, own_frames, height, columns, channels = video_clips.shape
        frames = tm * own_frames
        rows_all = height * space
        per = height // tm
        cells = frames * columns
        factor = float(clips * frames * rows_all * columns) ** (-0.5)
        own = conv_weights[0]
        taps = own.shape[0] // channels
        third = own.shape[0] // 3
        core = lax.axis_index("space") % 2

        early, late, clip = call(
            pick_kernel,
            [
                jax.ShapeDtypeStruct((third, channels), f32),
                jax.ShapeDtypeStruct((third // 2, channels), f32),
                jax.ShapeDtypeStruct(video_clips.shape[1:], f32),
            ],
            [pltpu.SemaphoreType.DMA((3,))],
            2,
            0,
            60,
            pltpu.HBM,
        )(video_clips, conv_weights)
        mine = send(early, swap_section)
        mine_late = send(late, swap_section)
        block = lax.all_gather(clip, "tm")
        bottom, top = block[:, :, height - 3 :], block[:, :, :3]
        to_inner = jnp.where(core == 0, bottom, top)
        to_outer = jnp.where(core == 0, top, bottom)
        inner = send(to_inner, swap_core)
        outer = send(to_outer, swap_outer)
        ready, _, _ = lax.optimization_barrier((mine, to_inner, to_outer))
        other = send(ready, swap_core)
        other_late = send(mine_late, swap_core)

        part = channels // tm
        dims = (tm, own_frames, height, rows_all, columns, channels, factor)
        field = (frames + 2, columns, channels)
        rows = height + 4
        products = 8 * 128 * channels * cells * 9
        shape = jax.ShapeDtypeStruct
        taken = shape((10 * channels, 6 * channels), bf16)
        encoder, decoder, turned, *begun = call(
            functools.partial(first_kernel, dims),
            [taken] * 3 + [shape((2,) + field, bf16)] * 2 + [shape((2, frames, columns, channels), f32)],
            [vmem((height,) + field, bf16)] * 2,
            6,
            0,
            24,
        )(block, own, mine, other, mine_late, other_late)

        *sent, xh, xl, lh, ll = call(
            functools.partial(activations_kernel, dims),
            [shape((2, part, per * cells), f32)] * tm
            + [shape((height + 6,) + field, bf16)] * 2
            + [shape((rows,) + field, bf16)] * 2,
            [
                vmem((height + 2, frames, columns, channels), f32),
                vmem((per + 2,) + field, bf16),
                vmem((per + 2,) + field, bf16),
                vmem((per + 4, frames, columns, channels), f32),
                vmem((2, channels, per * cells), f32),
            ],
            9,
            3 * products * (3 * per + 4),
            28,
        )(block, inner, outer, encoder, decoder, turned, *begun)

        extra = height - 1 - per
        more_high, more_low = call(
            functools.partial(latents_kernel, dims),
            [shape((extra,) + field, bf16)] * 2,
            [],
            3,
            3 * products * extra,
            12,
        )(xh, xl, encoder)
        pieces = [sent[0]] + [send(sent[k], later(k)) for k in range(1, tm)]
        width = part // (2 * pairs)
        grads = shape((2, pairs, taps, width, channels), f32)
        keep, give = call(
            functools.partial(
                weights_kernel, (tm, own_frames, height, rows_all, columns, channels, pairs)
            ),
            [grads, grads],
            [vmem((2, height, 6 * part, cells), bf16)] + [vmem((rows,) + field, bf16)] * 2,
            tm + 6,
            16 * taps * part * height * cells * channels,
            16,
        )(*pieces, xh, xl, lh, ll, more_high, more_low)

        both = keep + send(give, swap_core)
        total = both[0, 0]
        for flip in range(2):
            for step in range(pairs):
                if flip or step:
                    total = total + send(both[flip, step], across(flip, step))

        cut = 2 * taps // 3
        early, late = total[:cut], total[cut:]
        late_rows = [late] + [send(late, across(0, k)) for k in range(1, pairs)]
        early_all = [early] + [send(early, later(k)) for k in range(1, tm)]
        late_rows, early_all = jnp.stack(late_rows), jnp.stack(early_all)
        early_all = jnp.stack([early_all] + [send(early_all, across(0, k)) for k in range(1, pairs)])
        late_all = jnp.stack([late_rows] + [send(late_rows, later(k)) for k in range(1, tm)])
        early_all, late_all = lax.optimization_barrier((early_all, late_all))
        came = [send(x, swap_core) for x in (early_all, late_all)]
        out = call(
            functools.partial(assembled_kernel, (tm, pairs, channels)),
            jax.ShapeDtypeStruct(own.shape, f32),
            [],
            4,
            0,
            12,
        )(early_all, late_all, *came)
        return out[None]

    return local


def solution(mesh):
    return jax.shard_map(
        make_local(dict(mesh.shape)),
        mesh=mesh,
        in_specs=(P(None, "tm", "space", None, None), P("segment", None, None)),
        out_specs=P("segment", None, None),
        check_vma=False,
    )
```
